32 devices in a mesh: seg: 4 (over x, core), sec: 8 (over z, y).
Axes of the slice: x: 2, y: 2, z: 4, core: 2. Of those that a mesh axis runs over, the one named last changes fastest.
Arguments:
- wave: bfloat16 [4, 8, 256, 256], P('seg', 'sec'), may hold values from -21 to 21
- diag_energy: float32 [4, 8, 2, 256], P('seg'), may hold values from 0.5 to 4
- term_list: int32 [4, 768, 4], P('seg', 'sec'), may hold values from 0 to 15, as said below
- term_count: int32 [4, 8], P('seg', 'sec'), may hold values from 19 to 96, as said below
- term_coef: float32 [4, 768], P('seg', 'sec'), may hold values from -0.6 to 0.6
- edge_env: bfloat16 [4, 128, 256, 256], P('seg', 'sec'), may hold values from -0.375 to 0.375
- right_env: bfloat16 [4, 128, 256, 256], P('seg', 'sec'), may hold values from -0.375 to 0.375
Outputs:
- image0: float32 [4, 8, 256, 256], P('seg', 'sec')
- search: bfloat16 [4, 8, 256, 256], P('seg', 'sec')
- image1: float32 [4, 8, 256, 256], P('seg', 'sec')
The draws below stay inside these ranges and needn't reach their ends.
Inputs may be any that keep to these rules, and one draw needn't show every extreme that they name: `term_list`: columns 0 and 1 name blocks of the segment, 0 to 7; column 2 names a channel held by the same device, 0 to 15; column 3 is 0 or 1. Rows at or past a device's count hold arbitrary values in these ranges. `term_count`: the live terms of a device are its first rows; in every segment one device holds exactly 96.
All inputs are finite; a program needn't handle non-finite values.
Results may differ from the reference program's by a relative error of at most 0.00115.
The reference program's roundings to bfloat16 on the way count: a program that leaves them out, or rounds other values in their place, can miss the bound.
Values may be sent and summed in bfloat16 or wider, within the bound.
A program may use at most 128 MiB of HBM per device.

```python
import math
import jax
import jax.numpy as jnp
from jax import lax

SECTOR_DIM = 256
ENV_DEV = 16
TERMS_CAP = 96
SEGMENTS = 4
BLOCKS = 8
CHANNELS = 128
TERMS = 768
N_SEC = 8


def draw_wave(key, part):
    dims = (SEGMENTS, BLOCKS, SECTOR_DIM, SECTOR_DIM)
    position = jnp.arange(BLOCKS, dtype=jnp.float32)
    rising = 1.0 + 2.0 * position / max(BLOCKS - 1, 1)
    raw = jnp.clip(jax.random.normal(key, dims, jnp.float32), -5.0, 5.0)
    return (raw * rising[None, :, None, None]).astype(jnp.bfloat16)


def draw_term_list(key, part):
    dims = (SEGMENTS, TERMS)
    source = jax.random.randint(jax.random.fold_in(key, 1), dims, 0, BLOCKS)
    target = jax.random.randint(jax.random.fold_in(key, 2), dims, 0, BLOCKS)
    channel = jax.random.randint(jax.random.fold_in(key, 3), dims, 0, ENV_DEV)
    kinds = jax.random.randint(jax.random.fold_in(key, 4), dims, 0, 2)
    return jnp.stack([source, target, channel, kinds], axis=-1).astype(jnp.int32)


def draw_term_count(key, part):
    devices = TERMS // TERMS_CAP
    lowest = max(1, TERMS_CAP // 5)
    highest = 3 * TERMS_CAP // 5 + 1
    base = jax.random.randint(jax.random.fold_in(key, 11), (SEGMENTS, devices), lowest, highest)
    busiest = jax.random.randint(jax.random.fold_in(key, 12), (SEGMENTS, 1), 0, devices)
    marker = jnp.arange(devices, dtype=jnp.int32)[None, :] == busiest
    return jnp.where(marker, TERMS_CAP, base).astype(jnp.int32)


def levels(rng, shape, shards, low, high):
    level, own = 1.0, jax.random.fold_in(rng, 6)
    for axis_at, shards_of in shards:
        heights = jnp.exp(jax.random.uniform(jax.random.fold_in(own, axis_at), (shards_of,), jnp.float32, low / len(shards), high / len(shards)))
        level = level * jnp.repeat(heights, shape[axis_at] // shards_of).reshape([-1 if axis == axis_at else 1 for axis in range(len(shape))])
    return level


def centred(stream_key, shape, spread, bound, shards=(), kind=jnp.bfloat16):
    gain = levels(stream_key, shape, shards, -0.22, 0.18) if shards else 1.0
    entries = jax.random.normal(stream_key, shape, jnp.float32) * spread * gain
    return jnp.minimum(jnp.maximum(entries, -bound), bound).astype(kind)


def setup_inputs(seed: int = 0) -> dict:
    keys = jax.random.split(jax.random.key(seed), 8)
    return {
        "wave": draw_wave(jax.random.fold_in(keys[7], 71), 0),
        "diag_energy": jnp.clip(jnp.exp(math.log(4.0) - 2.0794415 * jax.random.uniform(keys[1], (SEGMENTS, BLOCKS, 2, SECTOR_DIM), jnp.float32) ** levels(keys[1], (SEGMENTS, BLOCKS, 2, SECTOR_DIM), ((0, 4),), -0.2, 0.2)), 0.5, 4.0),
        "term_list": draw_term_list(jax.random.fold_in(keys[7], 71), 0),
        "term_count": draw_term_count(jax.random.fold_in(keys[7], 71), 0),
        "term_coef": centred(keys[4], (SEGMENTS, TERMS), 0.1, 0.6, ((0, 4), (1, 8)), jnp.float32),
        "edge_env": centred(keys[5], (SEGMENTS, CHANNELS, SECTOR_DIM, SECTOR_DIM), SECTOR_DIM ** -0.5, 0.375, ((0, 4), (1, 8))),
        "right_env": centred(keys[6], (SEGMENTS, CHANNELS, SECTOR_DIM, SECTOR_DIM), SECTOR_DIM ** -0.5, 0.375, ((0, 4), (1, 8))),
    }


def apply_terms(gathered, left_env, right_env, term_rows, live_count, term_weights, totals):
    per_group = 16
    turn_count = (live_count + per_group - 1) // per_group

    def advance(turn, running):
        offset = (turn * per_group).astype(jnp.int32)
        picked = lax.dynamic_slice_in_dim(term_rows, offset, per_group, 0)
        weights = lax.dynamic_slice_in_dim(term_weights, offset, per_group, 0)
        active = offset + jnp.arange(per_group, dtype=jnp.int32) < live_count
        blocks = jnp.take(gathered, picked[:, 0], axis=0).astype(jnp.float32)
        right_part = jnp.take(right_env, picked[:, 2], axis=0).astype(jnp.float32)
        left_part = jnp.take(left_env, picked[:, 2], axis=0).astype(jnp.float32)
        product = jnp.einsum('gij,gjk->gik', blocks, right_part)
        rounded = product.astype(jnp.bfloat16).astype(jnp.float32)
        leftward = jnp.einsum('gij,gjk->gik', left_part, rounded)
        chosen = jnp.where((picked[:, 3] == 1)[:, None, None], leftward, product)
        scaled = chosen * jnp.where(active, weights, jnp.zeros_like(weights))[:, None, None]
        return running.at[picked[:, 1]].add(scaled)
    return lax.fori_loop(0, turn_count, advance, totals)

def apply_segment(gathered, left_env, right_env, term_rows, live_counts, term_weights):
    totals = jnp.zeros(gathered.shape, jnp.float32)

    def per_device(device, running):
        start = (device * TERMS_CAP).astype(jnp.int32)
        rows_here = lax.dynamic_slice_in_dim(term_rows, start, TERMS_CAP, 0)
        weights_here = lax.dynamic_slice_in_dim(term_weights, start, TERMS_CAP, 0)
        channel_shift = (jnp.arange(4, dtype=jnp.int32) == 2).astype(jnp.int32) * (device * ENV_DEV).astype(jnp.int32)
        return apply_terms(gathered, left_env, right_env, rows_here + channel_shift[None, :], live_counts[device], weights_here, running)
    return lax.fori_loop(0, N_SEC, per_device, totals)

def reference(wave, diag_energy, term_list, term_count, term_coef, edge_env, right_env):
    firsts, searches, seconds = ([], [], [])
    for segment in range(SEGMENTS):
        if segment > 0:
            left_env = edge_env[segment - 1]
        else:
            left_env = jnp.zeros(edge_env.shape[1:], jnp.bfloat16)
        right_here = right_env[segment]
        rows_here = term_list[segment]
        counts_here = term_count[segment]
        weights_here = term_coef[segment]
        current = wave[segment]
        image_first = apply_segment(current, left_env, right_here, rows_here, counts_here, weights_here)
        as_float = current.astype(jnp.float32)
        norm_wave = jnp.sum(as_float * as_float)
        rayleigh = jnp.sum(as_float * image_first)
        theta = rayleigh / norm_wave
        energy = diag_energy[segment]
        denominator = energy[:, 0, :, None] + energy[:, 1, None, :]
        correction = (image_first - theta * as_float) / denominator
        along = jnp.sum(as_float * correction)
        orthogonal = correction - along / norm_wave * as_float
        squared = jnp.sum(orthogonal * orthogonal)
        cells = current.size
        search_here = (orthogonal / jnp.sqrt(squared / cells + 1e-06)).astype(jnp.bfloat16)
        image_second = apply_segment(search_here, left_env, right_here, rows_here, counts_here, weights_here)
        firsts.append(image_first)
        searches.append(search_here)
        seconds.append(image_second)
    return (jnp.stack(firsts), jnp.stack(searches), jnp.stack(seconds))
```

```python
import functools

import jax
import jax.numpy as jnp
from jax import lax
from jax.experimental import pallas as pl
from jax.experimental.pallas import tpu as pltpu
from jax.sharding import PartitionSpec as P

STEP = 4
LEVELS = 32767.0
VM = pltpu.VMEM
SM = pltpu.SMEM


def shifted(value, axis, by):
    devices = lax.axis_size(axis)
    pairs = [(i, i + by) for i in range(devices) if 0 <= i + by < devices]
    return lax.ppermute(value, axis, pairs)


def partition(rows_ref, count_ref, coef_ref, packed_ref, weight_ref, many_ref):
    cap = packed_ref.shape[0] // 2

    def place(i, carry):
        n0, n1 = carry
        kind = rows_ref[i, 3]
        at = jnp.where(kind == 1, cap + n1, n0)
        packed_ref[at] = rows_ref[i, 0] + rows_ref[i, 1] * 256 + rows_ref[i, 2] * 65536
        weight_ref[at] = coef_ref[0, i]
        return n0 + 1 - kind, n1 + kind

    n0, n1 = lax.fori_loop(0, count_ref[0, 0], place, (jnp.int32(0), jnp.int32(0)))
    for extra in range(STEP):
        for at in (n0 + extra, cap + n1 + extra):
            packed_ref[at] = jnp.int32(0)
            weight_ref[at] = jnp.float32(0)
    many_ref[0] = n0
    many_ref[1] = n1


def fields(packed_ref, at):
    code = packed_ref[at]
    return code % 256, (code // 256) % 256, code // 65536


def add_plain(many, x_ref, right_ref, packed_ref, weight_ref, out_ref):
    def advance(turn, carry):
        done = []
        for u in range(STEP):
            at = turn * STEP + u
            src, tgt, chan = fields(packed_ref, at)
            product = jnp.dot(x_ref[src], right_ref[chan], preferred_element_type=jnp.float32)
            done.append((tgt, weight_ref[at], product))
        for tgt, weight, product in done:
            out_ref[tgt] += weight * product
        return carry

    lax.fori_loop(0, (many + STEP - 1) // STEP, advance, 0)


def add_left(many, x_ref, right_ref, left_ref, packed_ref, weight_ref, out_ref):
    cap = packed_ref.shape[0] // 2

    def advance(turn, carry):
        rounded = []
        for u in range(STEP):
            at = cap + turn * STEP + u
            src, tgt, chan = fields(packed_ref, at)
            product = jnp.dot(x_ref[src], right_ref[chan], preferred_element_type=jnp.float32)
            rounded.append((at, tgt, chan, product.astype(jnp.bfloat16)))
        done = []
        for at, tgt, chan, value in rounded:
            leftward = jnp.dot(left_ref[chan], value, preferred_element_type=jnp.float32)
            done.append((tgt, weight_ref[at], leftward))
        for tgt, weight, leftward in done:
            out_ref[tgt] += weight * leftward
        return carry

    lax.fori_loop(0, (many + STEP - 1) // STEP, advance, 0)


def plain_kernel(rows_ref, count_ref, coef_ref, x_ref, right_ref, out_ref, packed_ref, weight_ref, many_ref):
    partition(rows_ref, count_ref, coef_ref, packed_ref, weight_ref, many_ref)
    out_ref[...] = jnp.zeros_like(out_ref)
    add_plain(many_ref[0], x_ref, right_ref, packed_ref, weight_ref, out_ref)


def left_kernel(packed_ref, weight_ref, many_ref, x_ref, right_ref, left_ref, before_ref, out_ref):
    out_ref[...] = before_ref[...]
    add_left(many_ref[1], x_ref, right_ref, left_ref, packed_ref, weight_ref, out_ref)


def both_kernel(packed_ref, weight_ref, many_ref, x_ref, right_ref, left_ref, out_ref):
    out_ref[...] = jnp.zeros_like(out_ref)
    add_plain(many_ref[0], x_ref, right_ref, packed_ref, weight_ref, out_ref)
    add_left(many_ref[1], x_ref, right_ref, left_ref, packed_ref, weight_ref, out_ref)


def copy_to(src, dst, send_sem, recv_sem, device):
    return pltpu.make_async_remote_copy(
        src_ref=src,
        dst_ref=dst,
        send_sem=send_sem,
        recv_sem=recv_sem,
        device_id={"sec": device},
        device_id_type=pl.DeviceIdType.MESH,
    )


def greet_all(me, n):
    barrier = pltpu.get_barrier_semaphore()
    for s in range(1, n):
        pl.semaphore_signal(
            barrier, inc=1, device_id={"sec": (me + s) % n}, device_id_type=pl.DeviceIdType.MESH
        )
    pl.semaphore_wait(barrier, n - 1)


def gather(me, n, whole, sends, recvs):
    partner = me + 1 - 2 * (me % 2)

    def block(b, send, to):
        return copy_to(whole.at[b], whole.at[b], sends.at[send], recvs.at[b], to)

    for s in range(1, n // 2):
        block(me, s, (me + 2 * s) % n).start()
    block(me, 0, partner).start()
    for s in range(1, n // 2):
        came = (me + n - 2 * s) % n
        block(came, n // 2 + s, partner).wait_recv()
        block(came, n // 2 + s, partner).start()
    for s in range(n // 2):
        block((partner + n - 2 * s) % n, s, partner).wait_recv()
    for s in range(n // 2):
        block(me, s, partner).wait_send()
        if s:
            block(me, n // 2 + s, partner).wait_send()


def coded(value, code_ref, scale_ref):
    groups = value.reshape(value.shape[0] // 8, 8, value.shape[1])
    top = jnp.maximum(jnp.max(jnp.abs(groups), axis=0), 1e-30)
    scale_ref[...] = top * (1.0 / LEVELS)
    steps = jnp.round(groups * (LEVELS / top)[None])
    code_ref[...] = steps.reshape(value.shape).astype(jnp.int32).astype(jnp.int16)


def decoded(code_ref, scale_ref):
    code = code_ref[...].astype(jnp.int32).astype(jnp.float32)
    groups = code.reshape(code.shape[0] // 8, 8, code.shape[1]) * scale_ref[...][None]
    return groups.reshape(code.shape)


def reduce_scatter(me, n, partial, image, bufs):
    half = n // 2
    partner = me + 1 - 2 * (me % 2)
    (y_code, y_scale, y_code_in, y_scale_in, z_code, z_scale, z_code_in, z_scale_in, sems) = bufs

    def y_copies(s):
        return (
            copy_to(y_code.at[s], y_code_in.at[s], sems.at[0, s], sems.at[1, s], partner),
            copy_to(y_scale.at[s], y_scale_in.at[s], sems.at[2, s], sems.at[3, s], partner),
        )

    def z_copies(s):
        to = (me + 2 * s) % n
        return (
            copy_to(z_code.at[s], z_code_in.at[s], sems.at[4, s], sems.at[5, s], to),
            copy_to(z_scale.at[s], z_scale_in.at[s], sems.at[6, s], sems.at[7, s], to),
        )

    def send_y(t, carry):
        s = (t + 1) % half
        coded(partial[(partner + 2 * s) % n], y_code.at[s], y_scale.at[s])
        for copy in y_copies(s):
            copy.start()
        return carry

    lax.fori_loop(0, half, send_y, 0)

    def send_z(s, carry):
        for copy in y_copies(s):
            copy.wait_recv()
        total = partial[(me + 2 * s) % n] + decoded(y_code_in.at[s], y_scale_in.at[s])
        coded(total, z_code.at[s], z_scale.at[s])
        for copy in z_copies(s):
            copy.start()
        return carry

    lax.fori_loop(1, half, send_z, 0)
    for copy in y_copies(0):
        copy.wait_recv()
    image[0] = partial[me] + decoded(y_code_in.at[0], y_scale_in.at[0])

    def take_z(s, carry):
        for copy in z_copies(s):
            copy.wait_recv()
        image[0] += decoded(z_code_in.at[s], z_scale_in.at[s])
        return carry

    lax.fori_loop(1, half, take_z, 0)


def reduce_scatter_drain(me, n, bufs):
    half = n // 2
    partner = me + 1 - 2 * (me % 2)
    (y_code, y_scale, y_code_in, y_scale_in, z_code, z_scale, z_code_in, z_scale_in, sems) = bufs

    for s in range(half):
        copy_to(y_code.at[s], y_code_in.at[s], sems.at[0, s], sems.at[1, s], partner).wait_send()
        copy_to(y_scale.at[s], y_scale_in.at[s], sems.at[2, s], sems.at[3, s], partner).wait_send()
        if s:
            copy_to(z_code.at[s], z_code_in.at[s], sems.at[4, s], sems.at[5, s], partner).wait_send()
            copy_to(z_scale.at[s], z_scale_in.at[s], sems.at[6, s], sems.at[7, s], partner).wait_send()


def reduce_scratch(n, dim):
    half = n // 2
    pair = [VM((half, dim, dim), jnp.int16), VM((half, 8, dim), jnp.float32)]
    return pair * 4 + [pltpu.SemaphoreType.DMA((8, half))]


def total(value):
    return jnp.sum(jnp.sum(value, axis=0, keepdims=True), axis=1, keepdims=True)


def gather_kernel(n, mine_ref, whole_ref, sends, recvs):
    me = lax.axis_index("sec")
    greet_all(me, n)
    whole_ref[me] = mine_ref[0]
    gather(me, n, whole_ref, sends, recvs)


def step_kernel(
    n, partial_ref, wave_ref, energy_a_ref, energy_b_ref, image_ref, search_ref, whole_ref, inverse_ref, sums_ref, *rest
):
    *bufs, sum_sems, sends, recvs = rest
    dim = wave_ref.shape[1]
    me = lax.axis_index("sec")
    greet_all(me, n)
    reduce_scatter(me, n, partial_ref, image_ref, bufs)

    wave = wave_ref[0].astype(jnp.float32)
    inverse_ref[...] = 1.0 / (energy_a_ref[...] + energy_b_ref[...])
    wr = wave * inverse_ref[...]
    xx = total(wave * wave)
    b = total(wave * wr)
    r = total(wr * wr)
    safe = jnp.where(xx > 0, xx, 1.0)
    xh = total(wave * image_ref[0])
    theta_here = xh / safe
    c = image_ref[0] * inverse_ref[...] - theta_here * wr
    s = total(wave * c)
    alpha_here = s / safe
    v = c - alpha_here * wave
    p = total(v * v)
    q = total(v * wr)
    left_over = total(v * wave)
    row = lax.broadcasted_iota(jnp.int32, (8, 128), 0)
    tile = jnp.zeros((8, 128), jnp.float32)
    for i, value in enumerate((xx, xh, b, r, s, p, q, left_over)):
        tile = jnp.where(row == i, value, tile)
    sums_ref[me] = tile

    def sums_copy(slot, to, block):
        return copy_to(sums_ref.at[block], sums_ref.at[block], sum_sems.at[0, slot], sum_sems.at[1, slot], to)

    for slot in range(1, n):
        sums_copy(slot, (me + slot) % n, me).start()
    for slot in range(1, n):
        sums_copy(slot, (me + slot) % n, (me + n - slot) % n).wait_recv()
    xx_k, xh_k, b_k, r_k, s_k, p_k, q_k, l_k = (sums_ref[:, i, :] for i in range(8))
    safe_k = jnp.where(xx_k > 0, xx_k, 1.0)
    xx_all = jnp.sum(xx_k, axis=0, keepdims=True)
    theta = jnp.sum(xh_k, axis=0, keepdims=True) / xx_all
    d_theta = theta - xh_k / safe_k
    alpha = jnp.sum(s_k - d_theta * b_k, axis=0, keepdims=True) / xx_all
    d_alpha = alpha - s_k / safe_k
    tt_k = (
        p_k
        + d_theta * d_theta * r_k
        + d_alpha * d_alpha * xx_k
        - 2.0 * d_theta * q_k
        - 2.0 * d_alpha * l_k
        + 2.0 * d_theta * d_alpha * b_k
    )
    tt = jnp.maximum(jnp.sum(tt_k, axis=0, keepdims=True), 0.0)
    cells = n * dim * dim
    factor = (1.0 / jnp.sqrt(tt / cells + 1e-06))[:, :1]
    wave = wave_ref[0].astype(jnp.float32)
    theta, alpha = theta[:, :1], alpha[:, :1]
    orth = (image_ref[0] - theta * wave) * inverse_ref[...] - alpha * wave
    found = (orth * factor).astype(jnp.bfloat16)
    search_ref[0] = found
    whole_ref[me] = found
    gather(me, n, whole_ref, sends, recvs)
    for slot in range(1, n):
        sums_copy(slot, (me + slot) % n, me).wait_send()
    reduce_scatter_drain(me, n, bufs)


def reduce_kernel(n, partial_ref, image_ref, *bufs):
    me = lax.axis_index("sec")
    greet_all(me, n)
    reduce_scatter(me, n, partial_ref, image_ref, bufs)
    reduce_scatter_drain(me, n, bufs)


def vmem(k):
    return [pl.BlockSpec(memory_space=VM)] * k


def smem(k):
    return [pl.BlockSpec(memory_space=SM)] * k


def params(collective_id=None):
    if collective_id is None:
        return pltpu.CompilerParams(vmem_limit_bytes=40 << 20)
    return pltpu.CompilerParams(vmem_limit_bytes=48 << 20, collective_id=collective_id, has_side_effects=True)


def body(n, wave, diag_energy, term_list, term_count, term_coef, edge_env, right_env):
    mine = wave[0]
    dim = mine.shape[1]
    energy = diag_energy[0]
    left_env = shifted(edge_env, "seg", 1)[0]
    right_here = right_env[0]
    terms = term_list.shape[1]
    cap = (terms + STEP + 127) // 128 * 128
    dma = pltpu.SemaphoreType.DMA
    energy_mine = lax.dynamic_slice_in_dim(energy, lax.axis_index("sec"), 1, 0)[0]
    energy_a = energy_mine[0][:, None]
    energy_b = energy_mine[1][None, :]
    blocks_bf = jax.ShapeDtypeStruct((n, dim, dim), jnp.bfloat16)
    blocks_f = jax.ShapeDtypeStruct((n, dim, dim), jnp.float32)
    one_f = jax.ShapeDtypeStruct((1, dim, dim), jnp.float32)
    one_bf = jax.ShapeDtypeStruct((1, dim, dim), jnp.bfloat16)
    lists = (
        jax.ShapeDtypeStruct((2 * cap,), jnp.int32),
        jax.ShapeDtypeStruct((2 * cap,), jnp.float32),
        jax.ShapeDtypeStruct((2,), jnp.int32),
    )

    gathered = pl.pallas_call(
        functools.partial(gather_kernel, n),
        out_shape=blocks_bf,
        in_specs=vmem(1),
        out_specs=vmem(1)[0],
        scratch_shapes=[dma((n,)), dma((n,))],
        compiler_params=params(0),
    )(mine)
    cost = pl.CostEstimate(flops=terms * dim**3, bytes_accessed=8 << 20, transcendentals=0)
    first, packed, weight, many = pl.pallas_call(
        plain_kernel,
        out_shape=(blocks_f, *lists),
        in_specs=smem(3) + vmem(2),
        out_specs=(*vmem(1), *smem(3)),
        compiler_params=params(),
        cost_estimate=cost,
    )(term_list[0], term_count, term_coef, gathered, right_here)
    partial_first = pl.pallas_call(
        left_kernel,
        out_shape=blocks_f,
        in_specs=smem(3) + vmem(4),
        out_specs=vmem(1)[0],
        compiler_params=params(),
        cost_estimate=cost,
    )(packed, weight, many, gathered, right_here, left_env, first)
    image_first, search_mine, search_whole = pl.pallas_call(
        functools.partial(step_kernel, n),
        out_shape=(one_f, one_bf, blocks_bf),
        in_specs=vmem(4),
        out_specs=tuple(vmem(3)),
        scratch_shapes=[VM((dim, dim), jnp.float32), VM((n, 8, 128), jnp.float32)]
        + reduce_scratch(n, dim)
        + [dma((2, n)), dma((n,)), dma((n,))],
        compiler_params=params(1),
    )(partial_first, mine, energy_a, energy_b)
    partial_second = pl.pallas_call(
        both_kernel,
        out_shape=blocks_f,
        in_specs=smem(3) + vmem(3),
        out_specs=vmem(1)[0],
        compiler_params=params(),
        cost_estimate=cost,
    )(packed, weight, many, search_whole, right_here, left_env)
    image_second = pl.pallas_call(
        functools.partial(reduce_kernel, n),
        out_shape=one_f,
        in_specs=vmem(1),
        out_specs=vmem(1)[0],
        scratch_shapes=reduce_scratch(n, dim),
        compiler_params=params(2),
    )(partial_second)
    return (image_first[None], search_mine[None], image_second[None])


def solution(mesh):
    return jax.shard_map(
        functools.partial(body, mesh.shape["sec"]),
        mesh=mesh,
        in_specs=(
            P("seg", "sec", None, None),
            P("seg", None, None, None),
            P("seg", "sec", None),
            P("seg", "sec"),
            P("seg", "sec"),
            P("seg", "sec", None, None),
            P("seg", "sec", None, None),
        ),
        out_specs=(
            P("seg", "sec", None, None),
            P("seg", "sec", None, None),
            P("seg", "sec", None, None),
        ),
        check_vma=False,
    )
```

```python
import functools

import jax
import jax.numpy as jnp
from jax import lax
from jax.experimental import pallas as pl
from jax.experimental.pallas import tpu as pltpu
from jax.sharding import PartitionSpec as P

STEP = 4
PARTS = 4
CUTS = 2
LEVELS = 32767.0
VM = pltpu.VMEM
SM = pltpu.SMEM


def shifted(value, axis, by):
    devices = lax.axis_size(axis)
    pairs = [(i, i + by) for i in range(devices) if 0 <= i + by < devices]
    return lax.ppermute(value, axis, pairs)


def partition(rows_ref, count_ref, coef_ref, packed_ref, weight_ref, many_ref):
    cap = packed_ref.shape[0] // 2

    def place(i, carry):
        n0, n1 = carry
        kind = rows_ref[3, i]
        at = jnp.where(kind == 1, cap + n1, n0)
        packed_ref[at] = rows_ref[0, i] + rows_ref[1, i] * 256 + rows_ref[2, i] * 65536
        weight_ref[at] = coef_ref[0, i]
        return n0 + 1 - kind, n1 + kind

    n0, n1 = lax.fori_loop(0, count_ref[0, 0], place, (jnp.int32(0), jnp.int32(0)))
    for extra in range(STEP):
        for at in (n0 + extra, cap + n1 + extra):
            packed_ref[at] = jnp.int32(0)
            weight_ref[at] = jnp.float32(0)
    many_ref[0] = n0
    many_ref[1] = n1


def fields(packed_ref, at):
    code = packed_ref[at]
    return code % 256, (code // 256) % 256, code // 65536


def add_plain(many, x_ref, right_ref, packed_ref, weight_ref, out_ref):
    def advance(turn, carry):
        done = []
        for u in range(STEP):
            at = turn * STEP + u
            src, tgt, chan = fields(packed_ref, at)
            product = jnp.dot(x_ref[src], right_ref[chan], preferred_element_type=jnp.float32)
            done.append((tgt, weight_ref[at], product))
        for tgt, weight, product in done:
            out_ref[tgt] += weight * product
        return carry

    lax.fori_loop(0, (many + STEP - 1) // STEP, advance, 0)


def add_left(many, x_ref, right_ref, left_ref, packed_ref, weight_ref, out_ref):
    cap = packed_ref.shape[0] // 2

    def advance(turn, carry):
        rounded = []
        for u in range(STEP):
            at = cap + turn * STEP + u
            src, tgt, chan = fields(packed_ref, at)
            product = jnp.dot(x_ref[src], right_ref[chan], preferred_element_type=jnp.float32)
            rounded.append((at, tgt, chan, product.astype(jnp.bfloat16)))
        done = []
        for at, tgt, chan, value in rounded:
            leftward = jnp.dot(left_ref[chan], value, preferred_element_type=jnp.float32)
            done.append((tgt, weight_ref[at], leftward))
        for tgt, weight, leftward in done:
            out_ref[tgt] += weight * leftward
        return carry

    lax.fori_loop(0, (many + STEP - 1) // STEP, advance, 0)


def plain_kernel(rows_ref, count_ref, coef_ref, x_ref, right_ref, out_ref, packed_ref, weight_ref, many_ref):
    partition(rows_ref, count_ref, coef_ref, packed_ref, weight_ref, many_ref)
    out_ref[...] = jnp.zeros_like(out_ref)
    add_plain(many_ref[0], x_ref, right_ref, packed_ref, weight_ref, out_ref)


def left_kernel(packed_ref, weight_ref, many_ref, x_ref, right_ref, left_ref, before_ref, out_ref):
    out_ref[...] = before_ref[...]
    add_left(many_ref[1], x_ref, right_ref, left_ref, packed_ref, weight_ref, out_ref)


def both_kernel(packed_ref, weight_ref, many_ref, x_ref, right_ref, left_ref, image_ref, search_ref, *rest):
    out_ref, image_out_ref, search_out_ref, sems = rest
    copies = (
        pltpu.make_async_copy(image_ref, image_out_ref, sems.at[0]),
        pltpu.make_async_copy(search_ref, search_out_ref, sems.at[1]),
    )
    for copy in copies:
        copy.start()
    out_ref[...] = jnp.zeros_like(out_ref)
    add_plain(many_ref[0], x_ref, right_ref, packed_ref, weight_ref, out_ref)
    add_left(many_ref[1], x_ref, right_ref, left_ref, packed_ref, weight_ref, out_ref)
    for copy in copies:
        copy.wait()


def copy_to(src, dst, send_sem, recv_sem, device):
    return pltpu.make_async_remote_copy(
        src_ref=src,
        dst_ref=dst,
        send_sem=send_sem,
        recv_sem=recv_sem,
        device_id={"sec": device},
        device_id_type=pl.DeviceIdType.MESH,
    )


def greet_all(me, n):
    barrier = pltpu.get_barrier_semaphore()
    for s in range(1, n):
        pl.semaphore_signal(
            barrier, inc=1, device_id={"sec": (me + s) % n}, device_id_type=pl.DeviceIdType.MESH
        )
    pl.semaphore_wait(barrier, n - 1)


def gather(me, n, whole, sends, recvs, make_part):
    half = n // 2
    rows = whole.shape[1] // PARTS
    side, major = me % 2, me // 2
    partner = me + 1 - 2 * side
    rises, falls = major < half - 1, major > 0

    def piece(b, c, way, to):
        ref = whole.at[b, pl.ds(c * rows, rows)]
        return copy_to(ref, ref, sends.at[way, b, c], recvs.at[b, c], to)

    def up(b, c):
        return piece(b, c, 0, (me + 2) % n)

    def down(b, c):
        return piece(b, c, 1, (me + n - 2) % n)

    def across(b, c):
        return piece(b, c, 2, partner)

    def when(ok, action):
        pl.when(ok)(action)

    def reached(d):
        return ((up, rises, major - d, major >= d), (down, falls, major + d, major + d < half))

    for c in range(PARTS):
        make_part(pl.ds(c * rows, rows))
        across(me, c).start()
        when(rises, lambda: up(me, c).start())
        when(falls, lambda: down(me, c).start())
    for d in range(1, half):
        for c in range(PARTS):
            for onward, more, m, ok in reached(d):

                def take(c=c, onward=onward, more=more, b=2 * m + side):
                    across(b, c).wait_recv()
                    when(more, lambda: onward(b, c).start())
                    across(b, c).start()

                when(ok, take)
    for c in range(PARTS):
        across(partner, c).wait_recv()
    for d in range(1, half):
        for c in range(PARTS):
            for _, _, m, ok in reached(d):
                when(ok, lambda: across(2 * m + 1 - side, c).wait_recv())
    for c in range(PARTS):
        across(me, c).wait_send()
        when(rises, lambda: up(me, c).wait_send())
        when(falls, lambda: down(me, c).wait_send())
    for d in range(1, half):
        for c in range(PARTS):
            for onward, more, m, ok in reached(d):

                def settle(c=c, onward=onward, more=more, b=2 * m + side):
                    when(more, lambda: onward(b, c).wait_send())
                    across(b, c).wait_send()

                when(ok, settle)


def coded(value, code_ref, scale_ref):
    groups = value.reshape(value.shape[0] // 8, 8, value.shape[1])
    top = jnp.maximum(jnp.max(jnp.abs(groups), axis=0), 1e-30)
    scale_ref[...] = top * (1.0 / LEVELS)
    steps = jnp.round(groups * (LEVELS / top)[None])
    code_ref[...] = steps.reshape(value.shape).astype(jnp.int32).astype(jnp.int16)


def decoded(code_ref, scale_ref):
    code = code_ref[...].astype(jnp.int32).astype(jnp.float32)
    groups = code.reshape(code.shape[0] // 8, 8, code.shape[1]) * scale_ref[...][None]
    return groups.reshape(code.shape)


def reduce_copies(me, n, bufs):
    partner = me + 1 - 2 * (me % 2)
    (y_code, y_scale, y_code_in, y_scale_in, z_code, z_scale, z_code_in, z_scale_in, sems) = bufs

    def y_copies(t):
        return (
            copy_to(y_code.at[t], y_code_in.at[t], sems.at[0, t], sems.at[1, t], partner),
            copy_to(y_scale.at[t], y_scale_in.at[t], sems.at[2, t], sems.at[3, t], partner),
        )

    def z_copies(t):
        to = (me + 2 * (t // CUTS)) % n
        return (
            copy_to(z_code.at[t], z_code_in.at[t], sems.at[4, t], sems.at[5, t], to),
            copy_to(z_scale.at[t], z_scale_in.at[t], sems.at[6, t], sems.at[7, t], to),
        )

    return y_copies, z_copies


def reduce_scatter(me, n, partial, image, bufs, meanwhile=None):
    slots = n // 2 * CUTS
    rows = partial.shape[1] // CUTS
    partner = me + 1 - 2 * (me % 2)
    (y_code, y_scale, y_code_in, y_scale_in, z_code, z_scale, z_code_in, z_scale_in, sems) = bufs
    y_copies, z_copies = reduce_copies(me, n, bufs)

    def cut(t):
        return pl.ds(pl.multiple_of((t % CUTS) * rows, rows), rows)

    def send_y(i, carry):
        t = (i + CUTS) % slots
        coded(partial[(partner + 2 * (t // CUTS)) % n, cut(t)], y_code.at[t], y_scale.at[t])
        for copy in y_copies(t):
            copy.start()
        return carry

    lax.fori_loop(0, slots, send_y, 0)
    if meanwhile is not None:
        meanwhile()

    def send_z(t, carry):
        for copy in y_copies(t):
            copy.wait_recv()
        added = partial[(me + 2 * (t // CUTS)) % n, cut(t)] + decoded(y_code_in.at[t], y_scale_in.at[t])
        coded(added, z_code.at[t], z_scale.at[t])
        for copy in z_copies(t):
            copy.start()
        return carry

    lax.fori_loop(CUTS, slots, send_z, 0)

    def own(t, carry):
        for copy in y_copies(t):
            copy.wait_recv()
        image[0, cut(t)] = partial[me, cut(t)] + decoded(y_code_in.at[t], y_scale_in.at[t])
        return carry

    lax.fori_loop(0, CUTS, own, 0)

    def take_z(t, carry):
        for copy in z_copies(t):
            copy.wait_recv()
        image[0, cut(t)] += decoded(z_code_in.at[t], z_scale_in.at[t])
        return carry

    lax.fori_loop(CUTS, slots, take_z, 0)


def reduce_scatter_drain(me, n, bufs):
    slots = n // 2 * CUTS
    y_copies, z_copies = reduce_copies(me, n, bufs)

    def settle_y(t, carry):
        for copy in y_copies(t):
            copy.wait_send()
        return carry

    def settle_z(t, carry):
        for copy in z_copies(t):
            copy.wait_send()
        return carry

    lax.fori_loop(0, slots, settle_y, 0)
    lax.fori_loop(CUTS, slots, settle_z, 0)


def reduce_scratch(n, dim):
    slots = n // 2 * CUTS
    pair = [VM((slots, dim // CUTS, dim), jnp.int16), VM((slots, 8, dim), jnp.float32)]
    return pair * 4 + [pltpu.SemaphoreType.DMA((8, slots))]


def total(value):
    return jnp.sum(jnp.sum(value, axis=0, keepdims=True), axis=1, keepdims=True)


def gather_kernel(n, mine_ref, right_ref, whole_ref, right_near_ref, loaded, sends, recvs):
    me = lax.axis_index("sec")
    load = pltpu.make_async_copy(mine_ref.at[0], whole_ref.at[me], loaded.at[0])
    bring = pltpu.make_async_copy(right_ref, right_near_ref, loaded.at[1])
    load.start()
    bring.start()
    greet_all(me, n)
    load.wait()
    gather(me, n, whole_ref, sends, recvs, lambda rows: None)
    bring.wait()


def step_kernel(n, partial_ref, wave_ref, energy_ref, image_ref, search_ref, whole_ref, *rest):
    inverse_ref, scaled_ref, residual_ref, sums_ref, *bufs, sum_sems, sends, recvs = rest
    dim = wave_ref.shape[1]
    me = lax.axis_index("sec")
    greet_all(me, n)
    row = lax.broadcasted_iota(jnp.int32, (8, 128), 0)

    def wave_sums():
        wave = wave_ref[0].astype(jnp.float32)
        down = lax.broadcasted_iota(jnp.int32, (dim, dim), 0)
        along = lax.broadcasted_iota(jnp.int32, (dim, dim), 1)
        diagonal = jnp.where(down == along, energy_ref[me, 0:1, :], 0.0)
        energy = jnp.sum(diagonal, axis=1, keepdims=True) + energy_ref[me, 1:2, :]
        inverse = 1.0 / energy
        wr = wave * inverse
        inverse_ref[...] = inverse
        scaled_ref[...] = wr
        tile = jnp.zeros((8, 128), jnp.float32)
        for i, value in ((0, total(wave * wave)), (2, total(wave * wr)), (3, total(wr * wr))):
            tile = jnp.where(row == i, value, tile)
        sums_ref[me] = tile

    reduce_scatter(me, n, partial_ref, image_ref, bufs, wave_sums)

    wave = wave_ref[0].astype(jnp.float32)
    xx = sums_ref[me, 0:1, 0:1]
    safe = jnp.where(xx > 0, xx, 1.0)
    xh = total(wave * image_ref[0])
    theta_here = xh / safe
    c = image_ref[0] * inverse_ref[...] - theta_here * scaled_ref[...]
    residual_ref[...] = c
    s = total(wave * c)
    alpha_here = s / safe
    v = residual_ref[...] - alpha_here * wave_ref[0].astype(jnp.float32)
    p = total(v * v)
    q = total(v * scaled_ref[...])
    left_over = total(v * wave_ref[0].astype(jnp.float32))
    tile = sums_ref[me]
    for i, value in ((1, xh), (4, s), (5, p), (6, q), (7, left_over)):
        tile = jnp.where(row == i, value, tile)
    sums_ref[me] = tile

    def sums_copy(slot, to, block):
        return copy_to(sums_ref.at[block], sums_ref.at[block], sum_sems.at[0, slot], sum_sems.at[1, slot], to)

    for slot in range(1, n):
        sums_copy(slot, (me + slot) % n, me).start()
    for slot in range(1, n):
        sums_copy(slot, (me + slot) % n, (me + n - slot) % n).wait_recv()
    xx_k, xh_k, b_k, r_k, s_k, p_k, q_k, l_k = (sums_ref[:, i, :] for i in range(8))
    safe_k = jnp.where(xx_k > 0, xx_k, 1.0)
    xx_all = jnp.sum(xx_k, axis=0, keepdims=True)
    theta = jnp.sum(xh_k, axis=0, keepdims=True) / xx_all
    d_theta = theta - xh_k / safe_k
    alpha = jnp.sum(s_k - d_theta * b_k, axis=0, keepdims=True) / xx_all
    d_alpha = alpha - s_k / safe_k
    tt_k = (
        p_k
        + d_theta * d_theta * r_k
        + d_alpha * d_alpha * xx_k
        - 2.0 * d_theta * q_k
        - 2.0 * d_alpha * l_k
        + 2.0 * d_theta * d_alpha * b_k
    )
    tt = jnp.maximum(jnp.sum(tt_k, axis=0, keepdims=True), 0.0)
    cells = n * dim * dim
    factor = (1.0 / jnp.sqrt(tt / cells + 1e-06))[:, :1]
    theta, alpha = theta[:, :1], alpha[:, :1]

    def find(rows):
        part = wave_ref[0, rows].astype(jnp.float32)
        orth = (image_ref[0, rows] - theta * part) * inverse_ref[rows] - alpha * part
        found = (orth * factor).astype(jnp.bfloat16)
        search_ref[0, rows] = found
        whole_ref[me, rows] = found

    gather(me, n, whole_ref, sends, recvs, find)
    for slot in range(1, n):
        sums_copy(slot, (me + slot) % n, me).wait_send()
    reduce_scatter_drain(me, n, bufs)


def reduce_kernel(n, partial_ref, image_ref, *bufs):
    me = lax.axis_index("sec")
    greet_all(me, n)
    reduce_scatter(me, n, partial_ref, image_ref, bufs)
    reduce_scatter_drain(me, n, bufs)


def vmem(k):
    return [pl.BlockSpec(memory_space=VM)] * k


def smem(k):
    return [pl.BlockSpec(memory_space=SM)] * k


def params(blocks, collective_id=None):
    size = (4 << 20) + (blocks << 18)
    if collective_id is None:
        return pltpu.CompilerParams(vmem_limit_bytes=size)
    return pltpu.CompilerParams(vmem_limit_bytes=size, collective_id=collective_id, has_side_effects=True)


def body(n, wave, diag_energy, term_list, term_count, term_coef, edge_env, right_env):
    mine = wave[0]
    dim = mine.shape[1]
    energy = diag_energy[0]
    left_env = shifted(edge_env, "seg", 1)[0]
    right_here = right_env[0]
    terms = term_list.shape[1]
    cap = (terms + STEP + 127) // 128 * 128
    dma = pltpu.SemaphoreType.DMA
    blocks_bf = jax.ShapeDtypeStruct((n, dim, dim), jnp.bfloat16)
    blocks_f = jax.ShapeDtypeStruct((n, dim, dim), jnp.float32)
    one_f = jax.ShapeDtypeStruct((1, dim, dim), jnp.float32)
    one_bf = jax.ShapeDtypeStruct((1, dim, dim), jnp.bfloat16)
    lists = (
        jax.ShapeDtypeStruct((2 * cap,), jnp.int32),
        jax.ShapeDtypeStruct((2 * cap,), jnp.float32),
        jax.ShapeDtypeStruct((2,), jnp.int32),
    )

    envs = 2 * right_here.shape[0]
    gather_sems = [dma((3, n, PARTS)), dma((n, PARTS))]
    hbm = pl.BlockSpec(memory_space=pltpu.HBM)
    anywhere = pl.BlockSpec(memory_space=pl.ANY)
    gathered, right_near = pl.pallas_call(
        functools.partial(gather_kernel, n),
        out_shape=(blocks_bf, jax.ShapeDtypeStruct(right_here.shape, right_here.dtype)),
        in_specs=[hbm, hbm],
        out_specs=tuple(vmem(2)),
        scratch_shapes=[dma((2,))] + gather_sems,
        compiler_params=params(n + envs, 0),
    )(mine, right_here)
    cost = pl.CostEstimate(flops=terms * dim**3, bytes_accessed=8 << 20, transcendentals=0)
    first, packed, weight, many = pl.pallas_call(
        plain_kernel,
        out_shape=(blocks_f, *lists),
        in_specs=smem(3) + vmem(2),
        out_specs=(*vmem(1), *smem(3)),
        compiler_params=params(3 * n + envs),
        cost_estimate=cost,
    )(term_list[0].T, term_count, term_coef, gathered, right_near)
    partial_first = pl.pallas_call(
        left_kernel,
        out_shape=blocks_f,
        in_specs=smem(3) + vmem(4),
        out_specs=vmem(1)[0],
        compiler_params=params(3 * n + envs),
        cost_estimate=cost,
    )(packed, weight, many, gathered, right_near, left_env, first)
    image_first, search_mine, search_whole = pl.pallas_call(
        functools.partial(step_kernel, n),
        out_shape=(one_f, one_bf, blocks_bf),
        in_specs=vmem(3),
        out_specs=tuple(vmem(3)),
        scratch_shapes=[VM((dim, dim), jnp.float32)] * 3
        + [VM((n, 8, 128), jnp.float32)]
        + reduce_scratch(n, dim)
        + [dma((2, n))]
        + gather_sems,
        compiler_params=params(4 * n, 1),
    )(partial_first, mine, energy)
    partial_second, image_out, search_out = pl.pallas_call(
        both_kernel,
        out_shape=(blocks_f, one_f, one_bf),
        in_specs=smem(3) + vmem(3) + [anywhere] * 2,
        out_specs=(*vmem(1), hbm, hbm),
        scratch_shapes=[dma((2,))],
        compiler_params=params(3 * n + envs),
        cost_estimate=cost,
    )(packed, weight, many, search_whole, right_near, left_env, image_first, search_mine)
    image_second = pl.pallas_call(
        functools.partial(reduce_kernel, n),
        out_shape=one_f,
        in_specs=vmem(1),
        out_specs=vmem(1)[0],
        scratch_shapes=reduce_scratch(n, dim),
        compiler_params=params(3 * n, 2),
    )(partial_second)
    return (image_out[None], search_out[None], image_second[None])


def solution(mesh):
    return jax.shard_map(
        functools.partial(body, mesh.shape["sec"]),
        mesh=mesh,
        in_specs=(
            P("seg", "sec", None, None),
            P("seg", None, None, None),
            P("seg", "sec", None),
            P("seg", "sec"),
            P("seg", "sec"),
            P("seg", "sec", None, None),
            P("seg", "sec", None, None),
        ),
        out_specs=(
            P("seg", "sec", None, None),
            P("seg", "sec", None, None),
            P("seg", "sec", None, None),
        ),
        check_vma=False,
    )
```

```python
import functools

import jax
import jax.numpy as jnp
from jax import lax
from jax.experimental import pallas as pl
from jax.experimental.pallas import tpu as pltpu
from jax.sharding import PartitionSpec as P

STEP = 8
PARTS = 4
CUTS = 2
LEVELS = 32767.0
VM = pltpu.VMEM
SM = pltpu.SMEM


def shifted(value, axis, by):
    devices = lax.axis_size(axis)
    pairs = [(i, i + by) for i in range(devices) if 0 <= i + by < devices]
    return lax.ppermute(value, axis, pairs)


def partition(rows_ref, count_ref, coef_ref, packed_ref, weight_ref, many_ref):
    cap = packed_ref.shape[0] // 2

    def place(i, carry):
        n0, n1 = carry
        kind = rows_ref[3, i]
        at = jnp.where(kind == 1, cap + n1, n0)
        packed_ref[at] = rows_ref[0, i] + rows_ref[1, i] * 256 + rows_ref[2, i] * 65536
        weight_ref[at] = coef_ref[0, i]
        return n0 + 1 - kind, n1 + kind

    n0, n1 = lax.fori_loop(0, count_ref[0, 0], place, (jnp.int32(0), jnp.int32(0)))
    for extra in range(STEP):
        for at in (n0 + extra, cap + n1 + extra):
            packed_ref[at] = jnp.int32(0)
            weight_ref[at] = jnp.float32(0)
    many_ref[0] = n0
    many_ref[1] = n1


def fields(packed_ref, at):
    code = packed_ref[at]
    return code % 256, (code // 256) % 256, code // 65536


def add_step(plain, left, turn, x_ref, right_ref, left_ref, packed_ref, weight_ref, out_ref):
    cap = packed_ref.shape[0] // 2
    rounded, done = [], []
    if left:
        for u in range(STEP):
            at = cap + turn * STEP + u
            src, tgt, chan = fields(packed_ref, at)
            product = jnp.dot(x_ref[src], right_ref[chan], preferred_element_type=jnp.float32)
            rounded.append((tgt, chan, weight_ref[at], product.astype(jnp.bfloat16)))
    if plain:
        for u in range(STEP):
            at = turn * STEP + u
            src, tgt, chan = fields(packed_ref, at)
            product = jnp.dot(x_ref[src], right_ref[chan], preferred_element_type=jnp.float32)
            done.append((tgt, weight_ref[at], product))
    for tgt, chan, weight, value in rounded:
        leftward = jnp.dot(left_ref[chan], value, preferred_element_type=jnp.float32)
        done.append((tgt, weight, leftward))
    for tgt, weight, value in done:
        out_ref[tgt] += weight * value


def add_terms(first, last, plain, left, *refs):
    def advance(turn, carry):
        add_step(plain, left, turn, *refs)
        return carry

    lax.fori_loop(first, last, advance, 0)


def steps(many):
    return (many + STEP - 1) // STEP


def plain_kernel(rows_ref, count_ref, coef_ref, x_ref, right_ref, out_ref, packed_ref, weight_ref, many_ref):
    partition(rows_ref, count_ref, coef_ref, packed_ref, weight_ref, many_ref)
    out_ref[...] = jnp.zeros_like(out_ref)
    add_terms(0, steps(many_ref[0]), True, False, x_ref, right_ref, None, packed_ref, weight_ref, out_ref)


def left_kernel(packed_ref, weight_ref, many_ref, x_ref, right_ref, left_ref, before_ref, out_ref):
    out_ref[...] = before_ref[...]
    add_terms(0, steps(many_ref[1]), False, True, x_ref, right_ref, left_ref, packed_ref, weight_ref, out_ref)


def both_kernel(packed_ref, weight_ref, many_ref, x_ref, right_ref, left_ref, image_ref, search_ref, *rest):
    out_ref, image_out_ref, search_out_ref, sems = rest
    copies = (
        pltpu.make_async_copy(image_ref, image_out_ref, sems.at[0]),
        pltpu.make_async_copy(search_ref, search_out_ref, sems.at[1]),
    )
    for copy in copies:
        copy.start()
    out_ref[...] = jnp.zeros_like(out_ref)
    refs = (x_ref, right_ref, left_ref, packed_ref, weight_ref, out_ref)
    n0, n1 = steps(many_ref[0]), steps(many_ref[1])
    common = jnp.minimum(n0, n1)
    add_terms(0, common, True, True, *refs)
    add_terms(common, n0, True, False, *refs)
    add_terms(common, n1, False, True, *refs)
    for copy in copies:
        copy.wait()


def copy_to(src, dst, send_sem, recv_sem, device):
    return pltpu.make_async_remote_copy(
        src_ref=src,
        dst_ref=dst,
        send_sem=send_sem,
        recv_sem=recv_sem,
        device_id={"sec": device},
        device_id_type=pl.DeviceIdType.MESH,
    )


def greet_all(me, n):
    barrier = pltpu.get_barrier_semaphore()
    for s in range(1, n):
        pl.semaphore_signal(
            barrier, inc=1, device_id={"sec": (me + s) % n}, device_id_type=pl.DeviceIdType.MESH
        )
    pl.semaphore_wait(barrier, n - 1)


def gather(me, n, whole, sends, recvs, make_part):
    half = n // 2
    rows = whole.shape[1] // PARTS
    side, major = me % 2, me // 2
    partner = me + 1 - 2 * side
    rises, falls = major < half - 1, major > 0

    def piece(b, c, way, to):
        ref = whole.at[b, pl.ds(c * rows, rows)]
        return copy_to(ref, ref, sends.at[way, b, c], recvs.at[b, c], to)

    def up(b, c):
        return piece(b, c, 0, (me + 2) % n)

    def down(b, c):
        return piece(b, c, 1, (me + n - 2) % n)

    def across(b, c):
        return piece(b, c, 2, partner)

    def when(ok, action):
        pl.when(ok)(action)

    def reached(d):
        return ((up, rises, major - d, major >= d), (down, falls, major + d, major + d < half))

    for c in range(PARTS):
        make_part(pl.ds(c * rows, rows))
        across(me, c).start()
        when(rises, lambda: up(me, c).start())
        when(falls, lambda: down(me, c).start())
    for d in range(1, half):
        for c in range(PARTS):
            for onward, more, m, ok in reached(d):

                def take(c=c, onward=onward, more=more, b=2 * m + side):
                    across(b, c).wait_recv()
                    when(more, lambda: onward(b, c).start())
                    across(b, c).start()

                when(ok, take)
    for c in range(PARTS):
        across(partner, c).wait_recv()
    for d in range(1, half):
        for c in range(PARTS):
            for _, _, m, ok in reached(d):
                when(ok, lambda: across(2 * m + 1 - side, c).wait_recv())
    for c in range(PARTS):
        across(me, c).wait_send()
        when(rises, lambda: up(me, c).wait_send())
        when(falls, lambda: down(me, c).wait_send())
    for d in range(1, half):
        for c in range(PARTS):
            for onward, more, m, ok in reached(d):

                def settle(c=c, onward=onward, more=more, b=2 * m + side):
                    when(more, lambda: onward(b, c).wait_send())
                    across(b, c).wait_send()

                when(ok, settle)


def coded(value, code_ref, scale_ref):
    groups = value.reshape(value.shape[0] // 8, 8, value.shape[1])
    top = jnp.maximum(jnp.max(jnp.abs(groups), axis=0), 1e-30)
    scale_ref[...] = top * (1.0 / LEVELS)
    steps = jnp.round(groups * (LEVELS / top)[None])
    code_ref[...] = steps.reshape(value.shape).astype(jnp.int32).astype(jnp.int16)


def decoded(code_ref, scale_ref):
    code = code_ref[...].astype(jnp.int32).astype(jnp.float32)
    groups = code.reshape(code.shape[0] // 8, 8, code.shape[1]) * scale_ref[...][None]
    return groups.reshape(code.shape)


def reduce_copies(me, n, bufs):
    partner = me + 1 - 2 * (me % 2)
    (y_code, y_scale, y_code_in, y_scale_in, z_code, z_scale, z_code_in, z_scale_in, sems) = bufs

    def y_copies(t):
        return (
            copy_to(y_code.at[t], y_code_in.at[t], sems.at[0, t], sems.at[1, t], partner),
            copy_to(y_scale.at[t], y_scale_in.at[t], sems.at[2, t], sems.at[3, t], partner),
        )

    def z_copies(t):
        to = (me + 2 * (t // CUTS)) % n
        return (
            copy_to(z_code.at[t], z_code_in.at[t], sems.at[4, t], sems.at[5, t], to),
            copy_to(z_scale.at[t], z_scale_in.at[t], sems.at[6, t], sems.at[7, t], to),
        )

    return y_copies, z_copies


def reduce_scatter(me, n, partial, image, bufs, meanwhile=None):
    slots = n // 2 * CUTS
    rows = partial.shape[1] // CUTS
    partner = me + 1 - 2 * (me % 2)
    (y_code, y_scale, y_code_in, y_scale_in, z_code, z_scale, z_code_in, z_scale_in, sems) = bufs
    y_copies, z_copies = reduce_copies(me, n, bufs)

    def cut(t):
        return pl.ds(pl.multiple_of((t % CUTS) * rows, rows), rows)

    def send_y(i, carry):
        t = (i + CUTS) % slots
        coded(partial[(partner + 2 * (t // CUTS)) % n, cut(t)], y_code.at[t], y_scale.at[t])
        for copy in y_copies(t):
            copy.start()
        return carry

    lax.fori_loop(0, slots, send_y, 0)
    if meanwhile is not None:
        meanwhile()

    def send_z(t, carry):
        for copy in y_copies(t):
            copy.wait_recv()
        added = partial[(me + 2 * (t // CUTS)) % n, cut(t)] + decoded(y_code_in.at[t], y_scale_in.at[t])
        coded(added, z_code.at[t], z_scale.at[t])
        for copy in z_copies(t):
            copy.start()
        return carry

    lax.fori_loop(CUTS, slots, send_z, 0)

    def own(t, carry):
        for copy in y_copies(t):
            copy.wait_recv()
        image[0, cut(t)] = partial[me, cut(t)] + decoded(y_code_in.at[t], y_scale_in.at[t])
        return carry

    lax.fori_loop(0, CUTS, own, 0)

    def take_z(t, carry):
        for copy in z_copies(t):
            copy.wait_recv()
        image[0, cut(t)] += decoded(z_code_in.at[t], z_scale_in.at[t])
        return carry

    lax.fori_loop(CUTS, slots, take_z, 0)


def reduce_scatter_drain(me, n, bufs):
    slots = n // 2 * CUTS
    y_copies, z_copies = reduce_copies(me, n, bufs)

    def settle_y(t, carry):
        for copy in y_copies(t):
            copy.wait_send()
        return carry

    def settle_z(t, carry):
        for copy in z_copies(t):
            copy.wait_send()
        return carry

    lax.fori_loop(0, slots, settle_y, 0)
    lax.fori_loop(CUTS, slots, settle_z, 0)


def reduce_scratch(n, dim):
    slots = n // 2 * CUTS
    pair = [VM((slots, dim // CUTS, dim), jnp.int16), VM((slots, 8, dim), jnp.float32)]
    return pair * 4 + [pltpu.SemaphoreType.DMA((8, slots))]


def total(value):
    return jnp.sum(jnp.sum(value, axis=0, keepdims=True), axis=1, keepdims=True)


def gather_kernel(n, mine_ref, right_ref, whole_ref, right_near_ref, loaded, sends, recvs):
    me = lax.axis_index("sec")
    load = pltpu.make_async_copy(mine_ref.at[0], whole_ref.at[me], loaded.at[0])
    bring = pltpu.make_async_copy(right_ref, right_near_ref, loaded.at[1])
    load.start()
    bring.start()
    greet_all(me, n)
    load.wait()
    gather(me, n, whole_ref, sends, recvs, lambda rows: None)
    bring.wait()


def step_kernel(n, partial_ref, wave_ref, energy_ref, image_ref, search_ref, whole_ref, *rest):
    inverse_ref, scaled_ref, residual_ref, sums_ref, *bufs, sum_sems, sends, recvs = rest
    dim = wave_ref.shape[1]
    me = lax.axis_index("sec")
    greet_all(me, n)
    row = lax.broadcasted_iota(jnp.int32, (8, 128), 0)

    def wave_sums():
        wave = wave_ref[0].astype(jnp.float32)
        down = lax.broadcasted_iota(jnp.int32, (dim, dim), 0)
        along = lax.broadcasted_iota(jnp.int32, (dim, dim), 1)
        diagonal = jnp.where(down == along, energy_ref[me, 0:1, :], 0.0)
        energy = jnp.sum(diagonal, axis=1, keepdims=True) + energy_ref[me, 1:2, :]
        inverse = 1.0 / energy
        wr = wave * inverse
        inverse_ref[...] = inverse
        scaled_ref[...] = wr
        tile = jnp.zeros((8, 128), jnp.float32)
        for i, value in ((0, total(wave * wave)), (2, total(wave * wr)), (3, total(wr * wr))):
            tile = jnp.where(row == i, value, tile)
        sums_ref[me] = tile

    reduce_scatter(me, n, partial_ref, image_ref, bufs, wave_sums)

    wave = wave_ref[0].astype(jnp.float32)
    xx = sums_ref[me, 0:1, 0:1]
    safe = jnp.where(xx > 0, xx, 1.0)
    xh = total(wave * image_ref[0])
    theta_here = xh / safe
    c = image_ref[0] * inverse_ref[...] - theta_here * scaled_ref[...]
    residual_ref[...] = c
    s = total(wave * c)
    alpha_here = s / safe
    v = residual_ref[...] - alpha_here * wave_ref[0].astype(jnp.float32)
    p = total(v * v)
    q = total(v * scaled_ref[...])
    left_over = total(v * wave_ref[0].astype(jnp.float32))
    tile = sums_ref[me]
    for i, value in ((1, xh), (4, s), (5, p), (6, q), (7, left_over)):
        tile = jnp.where(row == i, value, tile)
    sums_ref[me] = tile

    def sums_copy(slot, to, block):
        return copy_to(sums_ref.at[block], sums_ref.at[block], sum_sems.at[0, slot], sum_sems.at[1, slot], to)

    for slot in range(1, n):
        sums_copy(slot, (me + slot) % n, me).start()
    for slot in range(1, n):
        sums_copy(slot, (me + slot) % n, (me + n - slot) % n).wait_recv()
    xx_k, xh_k, b_k, r_k, s_k, p_k, q_k, l_k = (sums_ref[:, i, :] for i in range(8))
    safe_k = jnp.where(xx_k > 0, xx_k, 1.0)
    xx_all = jnp.sum(xx_k, axis=0, keepdims=True)
    theta = jnp.sum(xh_k, axis=0, keepdims=True) / xx_all
    d_theta = theta - xh_k / safe_k
    alpha = jnp.sum(s_k - d_theta * b_k, axis=0, keepdims=True) / xx_all
    d_alpha = alpha - s_k / safe_k
    tt_k = (
        p_k
        + d_theta * d_theta * r_k
        + d_alpha * d_alpha * xx_k
        - 2.0 * d_theta * q_k
        - 2.0 * d_alpha * l_k
        + 2.0 * d_theta * d_alpha * b_k
    )
    tt = jnp.maximum(jnp.sum(tt_k, axis=0, keepdims=True), 0.0)
    cells = n * dim * dim
    factor = (1.0 / jnp.sqrt(tt / cells + 1e-06))[:, :1]
    theta, alpha = theta[:, :1], alpha[:, :1]

    def find(rows):
        part = wave_ref[0, rows].astype(jnp.float32)
        orth = (image_ref[0, rows] - theta * part) * inverse_ref[rows] - alpha * part
        found = (orth * factor).astype(jnp.bfloat16)
        search_ref[0, rows] = found
        whole_ref[me, rows] = found

    gather(me, n, whole_ref, sends, recvs, find)
    for slot in range(1, n):
        sums_copy(slot, (me + slot) % n, me).wait_send()
    reduce_scatter_drain(me, n, bufs)


def reduce_kernel(n, partial_ref, image_ref, *bufs):
    me = lax.axis_index("sec")
    greet_all(me, n)
    reduce_scatter(me, n, partial_ref, image_ref, bufs)
    reduce_scatter_drain(me, n, bufs)


def vmem(k):
    return [pl.BlockSpec(memory_space=VM)] * k


def smem(k):
    return [pl.BlockSpec(memory_space=SM)] * k


def params(blocks, collective_id=None):
    size = (4 << 20) + (blocks << 18)
    if collective_id is None:
        return pltpu.CompilerParams(vmem_limit_bytes=size)
    return pltpu.CompilerParams(vmem_limit_bytes=size, collective_id=collective_id, has_side_effects=True)


def body(n, wave, diag_energy, term_list, term_count, term_coef, edge_env, right_env):
    mine = wave[0]
    dim = mine.shape[1]
    energy = diag_energy[0]
    left_env = shifted(edge_env, "seg", 1)[0]
    right_here = right_env[0]
    terms = term_list.shape[1]
    cap = (terms + STEP + 127) // 128 * 128
    dma = pltpu.SemaphoreType.DMA
    blocks_bf = jax.ShapeDtypeStruct((n, dim, dim), jnp.bfloat16)
    blocks_f = jax.ShapeDtypeStruct((n, dim, dim), jnp.float32)
    one_f = jax.ShapeDtypeStruct((1, dim, dim), jnp.float32)
    one_bf = jax.ShapeDtypeStruct((1, dim, dim), jnp.bfloat16)
    lists = (
        jax.ShapeDtypeStruct((2 * cap,), jnp.int32),
        jax.ShapeDtypeStruct((2 * cap,), jnp.float32),
        jax.ShapeDtypeStruct((2,), jnp.int32),
    )

    envs = 2 * right_here.shape[0]
    gather_sems = [dma((3, n, PARTS)), dma((n, PARTS))]
    hbm = pl.BlockSpec(memory_space=pltpu.HBM)
    anywhere = pl.BlockSpec(memory_space=pl.ANY)
    gathered, right_near = pl.pallas_call(
        functools.partial(gather_kernel, n),
        out_shape=(blocks_bf, jax.ShapeDtypeStruct(right_here.shape, right_here.dtype)),
        in_specs=[hbm, hbm],
        out_specs=tuple(vmem(2)),
        scratch_shapes=[dma((2,))] + gather_sems,
        compiler_params=params(n + envs, 0),
    )(mine, right_here)
    cost = pl.CostEstimate(flops=terms * dim**3, bytes_accessed=8 << 20, transcendentals=0)
    first, packed, weight, many = pl.pallas_call(
        plain_kernel,
        out_shape=(blocks_f, *lists),
        in_specs=smem(3) + vmem(2),
        out_specs=(*vmem(1), *smem(3)),
        compiler_params=params(3 * n + envs),
        cost_estimate=cost,
    )(term_list[0].T, term_count, term_coef, gathered, right_near)
    partial_first = pl.pallas_call(
        left_kernel,
        out_shape=blocks_f,
        in_specs=smem(3) + vmem(4),
        out_specs=vmem(1)[0],
        compiler_params=params(3 * n + envs),
        cost_estimate=cost,
    )(packed, weight, many, gathered, right_near, left_env, first)
    image_first, search_mine, search_whole = pl.pallas_call(
        functools.partial(step_kernel, n),
        out_shape=(one_f, one_bf, blocks_bf),
        in_specs=vmem(3),
        out_specs=tuple(vmem(3)),
        scratch_shapes=[VM((dim, dim), jnp.float32)] * 3
        + [VM((n, 8, 128), jnp.float32)]
        + reduce_scratch(n, dim)
        + [dma((2, n))]
        + gather_sems,
        compiler_params=params(4 * n, 1),
    )(partial_first, mine, energy)
    partial_second, image_out, search_out = pl.pallas_call(
        both_kernel,
        out_shape=(blocks_f, one_f, one_bf),
        in_specs=smem(3) + vmem(3) + [anywhere] * 2,
        out_specs=(*vmem(1), hbm, hbm),
        scratch_shapes=[dma((2,))],
        compiler_params=params(3 * n + envs),
        cost_estimate=cost,
    )(packed, weight, many, search_whole, right_near, left_env, image_first, search_mine)
    image_second = pl.pallas_call(
        functools.partial(reduce_kernel, n),
        out_shape=one_f,
        in_specs=vmem(1),
        out_specs=vmem(1)[0],
        scratch_shapes=reduce_scratch(n, dim),
        compiler_params=params(3 * n, 2),
    )(partial_second)
    return (image_out[None], search_out[None], image_second[None])


def solution(mesh):
    return jax.shard_map(
        functools.partial(body, mesh.shape["sec"]),
        mesh=mesh,
        in_specs=(
            P("seg", "sec", None, None),
            P("seg", None, None, None),
            P("seg", "sec", None),
            P("seg", "sec"),
            P("seg", "sec"),
            P("seg", "sec", None, None),
            P("seg", "sec", None, None),
        ),
        out_specs=(
            P("seg", "sec", None, None),
            P("seg", "sec", None, None),
            P("seg", "sec", None, None),
        ),
        check_vma=False,
    )
```
